32 devices in a mesh: lat: 8 (over y, x, core), lon: 4 (over z).
Axes of the slice: x: 2, y: 2, z: 4, core: 2. Of those that a mesh axis runs over, the one named last changes fastest.
Arguments:
- field: bfloat16 [192, 384, 1440], P('lon', 'lat'), may hold values from -6 to 6
- cotangent: bfloat16 [192, 384, 1440], P('lon', 'lat'), may hold values from -6 to 6
- legendre: bfloat16 [384, 384, 384], P('lat', 'lon'), may hold values from -0.3125 to 0.3125
- spectral_weight: bfloat16 [384, 2, 192, 192], P('lon'), may hold values from -0.3125 to 0.3125
Outputs:
- output: bfloat16 [192, 384, 1440], P('lon', 'lat')
- field_grad: bfloat16 [192, 384, 1440], P('lon', 'lat')
- weight_grad: bfloat16 [384, 2, 192, 192], P('lon', None, 'lat')
The draws below stay inside these ranges and needn't reach their ends.
All inputs are finite; a program needn't handle non-finite values.
Results may differ from the reference program's by a relative error of at most 0.018.
Values may be sent and summed in bfloat16 or wider, within the bound.
A program may use at most 192 MiB of HBM per device.

```python
import math
import jax
import jax.numpy as jnp
from jax import lax

C = 192
NLAT = 384
NLON = 1440
M = 384
L = 384
N_LAT = 8
N_LON = 4


def level_of(own_key, extent, shards, least, high):
    def one(position, parts):
        draws = jax.random.uniform(jax.random.fold_in(jax.random.fold_in(own_key, 6), position), (parts,), jnp.float32, least / len(shards), high / len(shards))
        return jnp.repeat(jnp.exp(draws), extent[position] // parts).reshape((-1,) + (1,) * (len(extent) - position - 1))

    gain = one(*shards[0])
    for cut in shards[1:]:
        gain = gain * one(*cut)
    return gain


def bell_draw(stream_key, dims, scale, limit, pieces=(), kind=jnp.bfloat16):
    result = scale * jax.random.normal(stream_key, dims, jnp.float32)
    if pieces:
        result = result * level_of(stream_key, dims, pieces, -0.22, 0.18)
    return jnp.clip(result, -limit, limit).astype(kind)


def setup_inputs(seed: int = 0) -> dict:
    keys = jax.random.split(jax.random.key(seed), 5)
    return {
        "field": bell_draw(keys[0], (C, NLAT, NLON), 1.0, 6.0, ((0, 4), (1, 8))),
        "cotangent": bell_draw(keys[1], (C, NLAT, NLON), 1.0, 6.0, ((0, 4), (1, 8))),
        "legendre": bell_draw(keys[2], (M, L, NLAT), NLAT ** -0.5, 0.3125, ((0, 8), (1, 4))),
        "spectral_weight": bell_draw(keys[3], (L, 2, C, C), (2 * C) ** -0.5, 0.3125, ((0, 4),)),
    }


def dft_table(longitudes, wavenumbers):
    column = jnp.arange(longitudes, dtype=jnp.int32)[:, None]
    wave_index = jnp.arange(wavenumbers, dtype=jnp.int32)[None, :]
    phase = (column * wave_index % longitudes).astype(jnp.float32) * (2.0 * math.pi / longitudes)
    factor = 1.0 / math.sqrt(longitudes)
    return jnp.stack([jnp.cos(phase) * factor, -jnp.sin(phase) * factor], axis=1).astype(jnp.bfloat16)

def analyse(grid, fourier):
    channels, latitudes, longitudes = grid.shape
    flat = jnp.dot(grid.reshape(channels * latitudes, longitudes), fourier.reshape(longitudes, -1), preferred_element_type=jnp.float32)
    return flat.astype(jnp.bfloat16).reshape(channels, latitudes, 2, -1)

def synthesise(waves, fourier):
    channels, latitudes = (waves.shape[0], waves.shape[1])
    longitudes = fourier.shape[0]
    flat = jnp.dot(waves.reshape(channels * latitudes, -1), fourier.reshape(longitudes, -1).T, preferred_element_type=jnp.float32)
    return flat.reshape(channels, latitudes, longitudes)

def legendre_forward(waves, legendre):
    return jnp.einsum('cakm,mla->ckml', waves.astype(jnp.float32), legendre.astype(jnp.float32)).astype(jnp.bfloat16)

def legendre_inverse(spectrum, legendre, blocks):
    width = spectrum.shape[3] // blocks
    total = jnp.zeros((spectrum.shape[0], legendre.shape[2], 2, spectrum.shape[2]), jnp.float32)
    for block in range(blocks):
        lower = block * width
        partial_sum = jnp.einsum('ckml,mla->cakm', spectrum[:, :, :, lower:lower + width].astype(jnp.float32), legendre[:, lower:lower + width].astype(jnp.float32))
        rounded = lax.optimization_barrier(partial_sum.astype(jnp.bfloat16))
        total = total + rounded.astype(jnp.float32)
    return total.astype(jnp.bfloat16)

def mix_forward(spectrum, weight):
    real_in = spectrum[:, 0].astype(jnp.float32)
    imag_in = spectrum[:, 1].astype(jnp.float32)
    w_real = weight[:, 0].astype(jnp.float32)
    w_imag = weight[:, 1].astype(jnp.float32)
    real_out = jnp.einsum('ldc,cml->dml', w_real, real_in) - jnp.einsum('ldc,cml->dml', w_imag, imag_in)
    imag_out = jnp.einsum('ldc,cml->dml', w_real, imag_in) + jnp.einsum('ldc,cml->dml', w_imag, real_in)
    return jnp.stack([real_out, imag_out], axis=1).astype(jnp.bfloat16)

def mix_adjoint(grad_spec, weight):
    grad_real = grad_spec[:, 0].astype(jnp.float32)
    grad_imag = grad_spec[:, 1].astype(jnp.float32)
    w_real = weight[:, 0].astype(jnp.float32)
    w_imag = weight[:, 1].astype(jnp.float32)
    real_out = jnp.einsum('ldc,dml->cml', w_real, grad_real) + jnp.einsum('ldc,dml->cml', w_imag, grad_imag)
    imag_out = jnp.einsum('ldc,dml->cml', w_real, grad_imag) - jnp.einsum('ldc,dml->cml', w_imag, grad_real)
    return jnp.stack([real_out, imag_out], axis=1).astype(jnp.bfloat16)

def weight_term(grad_spec, spectrum):
    grad_real = grad_spec[:, 0].astype(jnp.float32)
    grad_imag = grad_spec[:, 1].astype(jnp.float32)
    real_in = spectrum[:, 0].astype(jnp.float32)
    imag_in = spectrum[:, 1].astype(jnp.float32)
    term_real = jnp.einsum('dml,cml->ldc', grad_real, real_in) + jnp.einsum('dml,cml->ldc', grad_imag, imag_in)
    term_imag = jnp.einsum('dml,cml->ldc', grad_imag, real_in) - jnp.einsum('dml,cml->ldc', grad_real, imag_in)
    return jnp.stack([term_real, term_imag], axis=1)

def reference(field, cotangent, legendre, spectral_weight):
    fourier = dft_table(field.shape[2], legendre.shape[0])
    waves = analyse(field, fourier)
    spectrum = legendre_forward(waves, legendre)
    mixed = mix_forward(spectrum, spectral_weight)
    back = legendre_inverse(mixed, legendre, N_LON)
    output = (field.astype(jnp.float32) + synthesise(back, fourier)).astype(jnp.bfloat16)
    grad_waves = analyse(cotangent, fourier)
    grad_spec = legendre_forward(grad_waves, legendre)
    width = M // N_LAT
    grad_total = jnp.zeros(spectral_weight.shape, jnp.float32)
    for block in range(N_LAT):
        lower = block * width
        term = weight_term(grad_spec[:, :, lower:lower + width], spectrum[:, :, lower:lower + width])
        rounded = lax.optimization_barrier(term.astype(jnp.bfloat16))
        grad_total = grad_total + rounded.astype(jnp.float32)
    weight_grad = grad_total.astype(jnp.bfloat16)
    grad_mixed = mix_adjoint(grad_spec, spectral_weight)
    grad_back = legendre_inverse(grad_mixed, legendre, N_LON)
    field_grad = (cotangent.astype(jnp.float32) + synthesise(grad_back, fourier)).astype(jnp.bfloat16)
    return (output, field_grad, weight_grad)
```

```python
import math

import jax
import jax.numpy as jnp
import numpy as np
from jax import lax
from jax.experimental import pallas as pl
from jax.experimental.pallas import tpu as pltpu
from jax.sharding import PartitionSpec as P


CHUNKS = 2


def wave_table(longitudes, wavenumbers):
    wave_index = np.arange(wavenumbers, dtype=np.int64)[:, None]
    column = np.arange(longitudes, dtype=np.int64)[None, :]
    phase = (column * wave_index % longitudes).astype(np.float32) * np.float32(
        2.0 * math.pi / longitudes
    )
    factor = np.float32(1.0 / math.sqrt(longitudes))
    table = np.stack([np.cos(phase) * factor, -np.sin(phase) * factor], axis=1)
    return table.reshape(2 * wavenumbers, longitudes).astype(jnp.bfloat16)


def swap(blocks, axis):
    return lax.all_to_all(blocks, axis, split_axis=0, concat_axis=0)


def group_of(count, most):
    return max(size for size in range(1, most + 1) if count % size == 0)


def limits(flops, moved):
    return dict(
        compiler_params=pltpu.CompilerParams(vmem_limit_bytes=40 * 1024 * 1024),
        cost_estimate=pl.CostEstimate(flops=flops, bytes_accessed=moved, transcendentals=0),
    )


def lanes(pieces):
    return jnp.concatenate(pieces, axis=1)


def tiles(count):
    return -(-count // 128)


def put(wide, where, value):
    count = value.shape[1]
    spare = 128 * wide.shape[0] - count
    if spare:
        value = lanes([value, jnp.zeros((value.shape[0], spare), value.dtype)])
    for t in range(wide.shape[0]):
        wide[t, where, :] = value[:, 128 * t : 128 * (t + 1)]


def take(wide, where, count):
    return lanes([wide[t, where, :] for t in range(wide.shape[0])])[:, :count]


def gather_rows_kernel(chan, got_ref, out_ref, wide):
    lats, count, _ = got_ref.shape
    rows = got_ref.shape[2] // chan
    loaded = [got_ref[p].astype(jnp.float32) for p in range(lats)]
    for c in range(chan):
        piece = lanes([part[:, c * rows : (c + 1) * rows] for part in loaded])
        put(wide, pl.ds(c, count, stride=chan), piece)
    for m in range(out_ref.shape[0]):
        own = pl.ds(2 * chan * m, 2 * chan)
        out_ref[m] = take(wide, own, out_ref.shape[2]).astype(out_ref.dtype)


def gather_rows(got, chan):
    lats, count, flat = got.shape
    rows = flat // chan
    waves = count // 2
    step_waves = 8 if waves % 8 == 0 else waves
    return pl.pallas_call(
        lambda *refs: gather_rows_kernel(chan, *refs),
        grid=(waves // step_waves,),
        in_specs=[pl.BlockSpec((lats, 2 * step_waves, flat), lambda step: (0, step, 0))],
        out_specs=pl.BlockSpec((step_waves, 2 * chan, lats * rows), lambda step: (step, 0, 0)),
        out_shape=jax.ShapeDtypeStruct((waves, 2 * chan, lats * rows), got.dtype),
        scratch_shapes=[pltpu.VMEM((tiles(lats * rows), 2 * step_waves * chan, 128), jnp.float32)],
        **limits(0, 4 * got.size),
    )(got)


def analyse_kernel(table_ref, waves_ref, out_ref):
    results = [
        lax.dot_general(
            table_ref[m], waves_ref[m], (((1,), (1,)), ((), ())), preferred_element_type=jnp.float32
        )
        for m in range(table_ref.shape[0])
    ]
    out_ref[...] = lanes(results).astype(out_ref.dtype).reshape(out_ref.shape)


def analyse(table, waves, lons, first):
    width, degrees, latitudes = table.shape
    parts = waves.shape[1]
    group = math.lcm(parts, 128) // parts
    group = group if width % group == 0 else width
    offset = first // group
    out = jax.ShapeDtypeStruct((lons, degrees // lons, width * parts), waves.dtype)
    return pl.pallas_call(
        analyse_kernel,
        grid=(width // group,),
        in_specs=[
            pl.BlockSpec((group, degrees, latitudes), lambda step: (step, 0, 0)),
            pl.BlockSpec((group, parts, latitudes), lambda step: (step + offset, 0, 0)),
        ],
        out_specs=pl.BlockSpec((lons, degrees // lons, group * parts), lambda step: (0, 0, step)),
        out_shape=out,
        **limits(
            2 * width * degrees * latitudes * parts,
            2 * width * (degrees * latitudes + (degrees + latitudes) * parts),
        ),
    )(table, waves)


def synthesise_kernel(chan, table_ref, got_ref, out_ref, wide):
    group = table_ref.shape[0]
    degrees = table_ref.shape[1]
    lats = out_ref.shape[0]
    latitudes = table_ref.shape[2]
    rows = latitudes // lats
    parts = 2 * chan
    mixed = got_ref[...].reshape(degrees, group * parts).astype(jnp.float32)
    for m in range(group):
        one = mixed[:, m * parts : (m + 1) * parts].astype(table_ref.dtype)
        back = lax.dot_general(
            one, table_ref[m], (((0,), (0,)), ((), ())), preferred_element_type=jnp.float32
        )
        put(wide, pl.ds(m * parts, parts), back)
    per = math.lcm(rows, 128) // rows
    per = per if chan % per == 0 else chan
    for c in range(0, chan, per):
        taken = [
            take(wide, pl.ds(c + i, 2 * group, stride=chan), latitudes) for i in range(per)
        ]
        for p in range(lats):
            piece = lanes([one[:, p * rows : (p + 1) * rows] for one in taken])
            out_ref[p, :, c * rows : (c + per) * rows] = piece.astype(out_ref.dtype)


def synthesise(table, got, lats, chan):
    width, degrees, latitudes = table.shape
    lons, degrees_here, flat = got.shape
    parts = 2 * chan
    group = 8 if width % 8 == 0 else width
    return pl.pallas_call(
        lambda *refs: synthesise_kernel(chan, *refs),
        grid=(width // group,),
        in_specs=[
            pl.BlockSpec((group, degrees, latitudes), lambda step: (step, 0, 0)),
            pl.BlockSpec((lons, degrees_here, group * parts), lambda step: (0, 0, step)),
        ],
        out_specs=pl.BlockSpec(
            (lats, 2 * group, chan * latitudes // lats), lambda step: (0, step, 0)
        ),
        out_shape=jax.ShapeDtypeStruct((lats, 2 * width, chan * latitudes // lats), got.dtype),
        scratch_shapes=[pltpu.VMEM((tiles(latitudes), group * parts, 128), jnp.float32)],
        **limits(
            2 * width * degrees * latitudes * parts,
            2 * width * (degrees * latitudes + (degrees + latitudes) * parts),
        ),
    )(table, got)


def mix_kernel(adjoint, got_ref, weight_ref, sent_ref, spec_ref, wide):
    sign = -1.0 if adjoint else 1.0
    inner = 0 if adjoint else 1
    lons, group, flat = got_ref.shape
    rows, total_chan = spec_ref.shape[1:]
    width = rows // 2
    chan = total_chan // lons
    loaded = [got_ref[q].astype(jnp.float32) for q in range(lons)]
    for m in range(width):
        for k in range(2):
            lower = (2 * m + k) * chan
            piece = lanes([part[:, lower : lower + chan] for part in loaded])
            put(wide, pl.ds(k * width + m, group, stride=rows), piece)
    for index in range(group):
        own = pl.ds(index * rows, rows)
        both = take(wide, own, total_chan).astype(spec_ref.dtype)
        spec_ref[index] = both
        by_real, by_imag = (
            lax.dot_general(
                both,
                weight_ref[index, part],
                (((1,), (inner,)), ((), ())),
                preferred_element_type=jnp.float32,
            )
            for part in range(2)
        )
        real_out = by_real[:width] - sign * by_imag[width:]
        imag_out = by_real[width:] + sign * by_imag[:width]
        put(wide, own, jnp.concatenate([real_out, imag_out], axis=0))
    per = math.lcm(2 * chan, 128) // (2 * chan)
    per = per if width % per == 0 else width
    for m in range(0, width, per):
        taken = [
            take(wide, pl.ds(k * width + m + i, group, stride=rows), total_chan)
            for i in range(per)
            for k in range(2)
        ]
        for q in range(lons):
            piece = lanes([one[:, q * chan : (q + 1) * chan] for one in taken])
            lower = 2 * m * chan
            sent_ref[q, :, lower : lower + 2 * per * chan] = piece.astype(sent_ref.dtype)


def mix(got, weight, adjoint):
    lons, degrees, flat = got.shape
    total_chan = weight.shape[2]
    rows = flat * lons // total_chan
    group = 16 if degrees % 16 == 0 else degrees
    return pl.pallas_call(
        lambda *refs: mix_kernel(adjoint, *refs),
        grid=(degrees // group,),
        in_specs=[
            pl.BlockSpec((lons, group, flat), lambda step: (0, step, 0)),
            pl.BlockSpec((group, 2, total_chan, total_chan), lambda step: (step, 0, 0, 0)),
        ],
        out_specs=[
            pl.BlockSpec((lons, group, flat), lambda step: (0, step, 0)),
            pl.BlockSpec((group, rows, total_chan), lambda step: (step, 0, 0)),
        ],
        out_shape=[
            jax.ShapeDtypeStruct(got.shape, got.dtype),
            jax.ShapeDtypeStruct((degrees, rows, total_chan), got.dtype),
        ],
        scratch_shapes=[pltpu.VMEM((tiles(total_chan), group * rows, 128), jnp.float32)],
        **limits(4 * degrees * rows * total_chan**2, 2 * (weight.size + 3 * got.size)),
    )(got, weight)


def term_kernel(chunks, *refs):
    out_ref = refs[-1]
    chan = out_ref.shape[0]

    def over_rows(left, right):
        return lax.dot_general(
            left, right, (((0,), (0,)), ((), ())), preferred_element_type=jnp.float32
        )

    for index in range(refs[0].shape[0]):
        real_term = jnp.zeros((chan, chan), jnp.float32)
        imag_term = jnp.zeros((chan, chan), jnp.float32)
        for chunk in range(chunks):
            spec = refs[chunk][index]
            grad = refs[chunks + chunk][index]
            half = spec.shape[0] // 2
            wide = spec.astype(jnp.float32)
            turned = jnp.concatenate([-wide[half:], wide[:half]], axis=0).astype(spec.dtype)
            real_term += over_rows(grad, spec)
            imag_term += over_rows(grad, turned)
        both = jnp.concatenate([real_term, imag_term], axis=1)
        out_ref[:, 2 * chan * index : 2 * chan * (index + 1)] = both.astype(out_ref.dtype)


def weight_terms(specs, grads):
    degrees, rows, chan = specs[0].shape
    chunks = len(specs)
    group = group_of(degrees, 8)
    return pl.pallas_call(
        lambda *refs: term_kernel(chunks, *refs),
        grid=(degrees // group,),
        in_specs=[pl.BlockSpec((group, rows, chan), lambda step: (step, 0, 0))] * (2 * chunks),
        out_specs=pl.BlockSpec((chan, group * 2 * chan), lambda step: (0, step)),
        out_shape=jax.ShapeDtypeStruct((chan, degrees * 2 * chan), specs[0].dtype),
        compiler_params=pltpu.CompilerParams(vmem_limit_bytes=32 * 1024 * 1024),
        cost_estimate=pl.CostEstimate(
            flops=4 * chunks * degrees * rows * chan * chan,
            bytes_accessed=4 * degrees * chan * (chunks * rows + chan),
            transcendentals=0,
        ),
    )(*specs, *grads)


def on_device(field, cotangent, legendre, spectral_weight):
    lats = lax.axis_size("lat")
    lons = lax.axis_size("lon")
    chan, rows, longitudes = field.shape
    waves_here, degrees_here, latitudes = legendre.shape
    total_chan = chan * lons
    degrees = degrees_here * lons
    total_waves = waves_here * lats
    chunks = CHUNKS if waves_here % (8 * CHUNKS) == 0 else 1
    width = waves_here // chunks
    fourier = jnp.asarray(wave_table(longitudes, total_waves))
    f32 = jnp.float32
    bf16 = jnp.bfloat16

    tables = [
        lax.all_gather(legendre[j * width : (j + 1) * width], "lon", axis=1, tiled=True)
        for j in range(chunks)
    ]

    def to_waves(grid):
        flat = grid.reshape(chan * rows, longitudes)
        local = lax.dot_general(fourier, flat, (((1,), (1,)), ((), ())), preferred_element_type=f32)
        local = local.astype(bf16).reshape(lats, waves_here * 2, chan * rows)
        return gather_rows(swap(local, "lat"), chan)

    def to_grid(parts):
        got = jnp.concatenate(parts, axis=1)
        return lax.dot_general(
            got.reshape(total_waves * 2, chan * rows),
            fourier,
            (((0,), (0,)), ((), ())),
            preferred_element_type=f32,
        ).reshape(chan, rows, longitudes)

    def finish(mixed, table):
        return swap(synthesise(table, swap(mixed, "lon"), lats, chan), "lat")

    waves = to_waves(field)
    grad_waves = to_waves(cotangent)
    specs, grads, backs, grad_backs = [], [], [], []
    ready = None
    for j in range(chunks):
        table = tables[j]
        if ready is None:
            table, waves, grad_waves = lax.optimization_barrier((table, waves, grad_waves))
        else:
            table, mixed, grad_mixed = lax.optimization_barrier((table, *ready))
        got = swap(analyse(table, waves, lons, j * width), "lon")
        grad_got = swap(analyse(table, grad_waves, lons, j * width), "lon")
        if ready is not None:
            backs.append(finish(mixed, tables[j - 1]))
            grad_backs.append(finish(grad_mixed, tables[j - 1]))
        mixed, spec = mix(got, spectral_weight, False)
        grad_mixed, grad = mix(grad_got, spectral_weight, True)
        specs.append(spec)
        grads.append(grad)
        ready = (mixed, grad_mixed)
    backs.append(finish(mixed, table))
    grad_backs.append(finish(grad_mixed, table))
    terms = weight_terms(specs, grads)
    summed = lax.psum_scatter(terms, "lat", scatter_dimension=0, tiled=True)
    weight_grad = summed.reshape(-1, degrees_here, 2, total_chan).transpose(1, 2, 0, 3)
    output = (field.astype(f32) + to_grid(backs)).astype(bf16)
    field_grad = (cotangent.astype(f32) + to_grid(grad_backs)).astype(bf16)
    return (output, field_grad, weight_grad)


def solution(mesh):
    placed = (
        P("lon", "lat", None),
        P("lon", "lat", None),
        P("lat", "lon", None),
        P("lon", None, None, None),
    )
    return jax.shard_map(
        on_device,
        mesh=mesh,
        in_specs=placed,
        out_specs=(P("lon", "lat", None), P("lon", "lat", None), P("lon", None, "lat", None)),
        check_vma=False,
    )
```

```python
import math

import jax
import jax.numpy as jnp
import numpy as np
from jax import lax
from jax.experimental import pallas as pl
from jax.experimental.pallas import tpu as pltpu
from jax.sharding import PartitionSpec as P


def wave_table(longitudes, wavenumbers):
    wave_index = np.arange(wavenumbers, dtype=np.int64)[:, None]
    column = np.arange(longitudes, dtype=np.int64)[None, :]
    phase = (column * wave_index % longitudes).astype(np.float32) * np.float32(
        2.0 * math.pi / longitudes
    )
    factor = np.float32(1.0 / math.sqrt(longitudes))
    table = np.stack([np.cos(phase) * factor, -np.sin(phase) * factor], axis=1)
    return table.reshape(2 * wavenumbers, longitudes).astype(jnp.bfloat16)


def swap(blocks, axis):
    return lax.all_to_all(blocks, axis, split_axis=0, concat_axis=0)


def group_of(count, most):
    return max(size for size in range(1, most + 1) if count % size == 0)


def exchange_kernel(axes, *refs):
    count = len(axes)
    given, taken = refs[:count], refs[count : 2 * count]
    send_sems, recv_sems, own_sems = refs[2 * count :]
    barrier = pltpu.get_barrier_semaphore()
    greeted = 0
    for axis in sorted(set(axes)):
        size = lax.axis_size(axis)
        me = lax.axis_index(axis)
        for shift in range(1, size):
            peer = lax.rem(me + shift, size)
            pl.semaphore_signal(
                barrier, inc=1, device_id={axis: peer}, device_id_type=pl.DeviceIdType.MESH
            )
        greeted += size - 1
    pl.semaphore_wait(barrier, greeted)
    copies = []
    for index, axis in enumerate(axes):
        size = lax.axis_size(axis)
        me = lax.axis_index(axis)
        for shift in sorted(range(1, size), key=lambda d: -min(d, size - d)):
            peer = lax.rem(me + shift, size)
            copy = pltpu.make_async_remote_copy(
                src_ref=given[index].at[peer],
                dst_ref=taken[index].at[me],
                send_sem=send_sems.at[index, shift],
                recv_sem=recv_sems.at[index, shift],
                device_id={axis: peer},
                device_id_type=pl.DeviceIdType.MESH,
            )
            copy.start()
            copies.append(copy)
        own = pltpu.make_async_copy(
            given[index].at[me], taken[index].at[me], own_sems.at[index]
        )
        own.start()
        copies.append(own)
    for copy in copies:
        copy.wait()


def exchange(number, *pairs):
    arrays = [array for array, _ in pairs]
    axes = tuple(axis for _, axis in pairs)
    most = max(lax.axis_size(axis) for axis in axes)
    count = len(arrays)
    return pl.pallas_call(
        lambda *refs: exchange_kernel(axes, *refs),
        in_specs=[pl.BlockSpec(memory_space=pl.ANY)] * count,
        out_specs=[pl.BlockSpec(memory_space=pl.ANY)] * count,
        out_shape=[jax.ShapeDtypeStruct(array.shape, array.dtype) for array in arrays],
        scratch_shapes=[
            pltpu.SemaphoreType.DMA((count, most)),
            pltpu.SemaphoreType.DMA((count, most)),
            pltpu.SemaphoreType.DMA((count,)),
        ],
        compiler_params=pltpu.CompilerParams(collective_id=number, has_side_effects=True),
        cost_estimate=pl.CostEstimate(
            flops=0, bytes_accessed=64 * sum(array.size for array in arrays), transcendentals=0
        ),
    )(*arrays)


def limits(flops, moved):
    return dict(
        compiler_params=pltpu.CompilerParams(vmem_limit_bytes=40 * 1024 * 1024),
        cost_estimate=pl.CostEstimate(flops=flops, bytes_accessed=moved, transcendentals=0),
    )


def lanes(pieces):
    return jnp.concatenate(pieces, axis=1)


def tiles(count):
    return -(-count // 128)


def put(wide, where, value):
    count = value.shape[1]
    spare = 128 * wide.shape[0] - count
    if spare:
        value = lanes([value, jnp.zeros((value.shape[0], spare), value.dtype)])
    for t in range(wide.shape[0]):
        wide[t, where, :] = value[:, 128 * t : 128 * (t + 1)]


def take(wide, where, count):
    return lanes([wide[t, where, :] for t in range(wide.shape[0])])[:, :count]


def gather_rows_kernel(chan, got_ref, out_ref, wide):
    lats, count, _ = got_ref.shape
    rows = got_ref.shape[2] // chan
    loaded = [got_ref[p].astype(jnp.float32) for p in range(lats)]
    for c in range(chan):
        piece = lanes([part[:, c * rows : (c + 1) * rows] for part in loaded])
        put(wide, pl.ds(c, count, stride=chan), piece)
    for m in range(out_ref.shape[0]):
        own = pl.ds(2 * chan * m, 2 * chan)
        out_ref[m] = take(wide, own, out_ref.shape[2]).astype(out_ref.dtype)


def gather_rows(got, chan):
    lats, count, flat = got.shape
    rows = flat // chan
    waves = count // 2
    step_waves = 8 if waves % 8 == 0 else waves
    return pl.pallas_call(
        lambda *refs: gather_rows_kernel(chan, *refs),
        grid=(waves // step_waves,),
        in_specs=[pl.BlockSpec((lats, 2 * step_waves, flat), lambda step: (0, step, 0))],
        out_specs=pl.BlockSpec((step_waves, 2 * chan, lats * rows), lambda step: (step, 0, 0)),
        out_shape=jax.ShapeDtypeStruct((waves, 2 * chan, lats * rows), got.dtype),
        scratch_shapes=[pltpu.VMEM((tiles(lats * rows), 2 * step_waves * chan, 128), jnp.float32)],
        **limits(0, 4 * got.size),
    )(got)


def analyse_kernel(table_ref, waves_ref, out_ref):
    results = [
        lax.dot_general(
            table_ref[m], waves_ref[m], (((1,), (1,)), ((), ())), preferred_element_type=jnp.float32
        )
        for m in range(table_ref.shape[0])
    ]
    out_ref[...] = lanes(results).astype(out_ref.dtype).reshape(out_ref.shape)


def analyse(table, waves, lons, first):
    width, degrees, latitudes = table.shape
    parts = waves.shape[1]
    group = math.lcm(parts, 128) // parts
    group = group if width % group == 0 else width
    offset = first // group
    out = jax.ShapeDtypeStruct((lons, degrees // lons, width * parts), waves.dtype)
    return pl.pallas_call(
        analyse_kernel,
        grid=(width // group,),
        in_specs=[
            pl.BlockSpec((group, degrees, latitudes), lambda step: (step, 0, 0)),
            pl.BlockSpec((group, parts, latitudes), lambda step: (step + offset, 0, 0)),
        ],
        out_specs=pl.BlockSpec((lons, degrees // lons, group * parts), lambda step: (0, 0, step)),
        out_shape=out,
        **limits(
            2 * width * degrees * latitudes * parts,
            2 * width * (degrees * latitudes + (degrees + latitudes) * parts),
        ),
    )(table, waves)


def synthesise_kernel(chan, table_ref, got_ref, out_ref, wide):
    group = table_ref.shape[0]
    degrees = table_ref.shape[1]
    lats = out_ref.shape[0]
    latitudes = table_ref.shape[2]
    rows = latitudes // lats
    parts = 2 * chan
    mixed = got_ref[...].reshape(degrees, group * parts).astype(jnp.float32)
    for m in range(group):
        one = mixed[:, m * parts : (m + 1) * parts].astype(table_ref.dtype)
        back = lax.dot_general(
            one, table_ref[m], (((0,), (0,)), ((), ())), preferred_element_type=jnp.float32
        )
        put(wide, pl.ds(m * parts, parts), back)
    per = math.lcm(rows, 128) // rows
    per = per if chan % per == 0 else chan
    for c in range(0, chan, per):
        taken = [
            take(wide, pl.ds(c + i, 2 * group, stride=chan), latitudes) for i in range(per)
        ]
        for p in range(lats):
            piece = lanes([one[:, p * rows : (p + 1) * rows] for one in taken])
            out_ref[p, :, c * rows : (c + per) * rows] = piece.astype(out_ref.dtype)


def synthesise(table, got, lats, chan):
    width, degrees, latitudes = table.shape
    lons, degrees_here, flat = got.shape
    parts = 2 * chan
    group = 8 if width % 8 == 0 else width
    return pl.pallas_call(
        lambda *refs: synthesise_kernel(chan, *refs),
        grid=(width // group,),
        in_specs=[
            pl.BlockSpec((group, degrees, latitudes), lambda step: (step, 0, 0)),
            pl.BlockSpec((lons, degrees_here, group * parts), lambda step: (0, 0, step)),
        ],
        out_specs=pl.BlockSpec(
            (lats, 2 * group, chan * latitudes // lats), lambda step: (0, step, 0)
        ),
        out_shape=jax.ShapeDtypeStruct((lats, 2 * width, chan * latitudes // lats), got.dtype),
        scratch_shapes=[pltpu.VMEM((tiles(latitudes), group * parts, 128), jnp.float32)],
        **limits(
            2 * width * degrees * latitudes * parts,
            2 * width * (degrees * latitudes + (degrees + latitudes) * parts),
        ),
    )(table, got)


def mix_kernel(adjoint, got_ref, weight_ref, sent_ref, spec_ref, wide):
    sign = -1.0 if adjoint else 1.0
    inner = 0 if adjoint else 1
    lons, group, flat = got_ref.shape
    rows, total_chan = spec_ref.shape[1:]
    width = rows // 2
    chan = total_chan // lons
    loaded = [got_ref[q].astype(jnp.float32) for q in range(lons)]
    for m in range(width):
        for k in range(2):
            lower = (2 * m + k) * chan
            piece = lanes([part[:, lower : lower + chan] for part in loaded])
            put(wide, pl.ds(k * width + m, group, stride=rows), piece)
    for index in range(group):
        own = pl.ds(index * rows, rows)
        both = take(wide, own, total_chan).astype(spec_ref.dtype)
        spec_ref[index] = both
        by_real, by_imag = (
            lax.dot_general(
                both,
                weight_ref[index, part],
                (((1,), (inner,)), ((), ())),
                preferred_element_type=jnp.float32,
            )
            for part in range(2)
        )
        real_out = by_real[:width] - sign * by_imag[width:]
        imag_out = by_real[width:] + sign * by_imag[:width]
        put(wide, own, jnp.concatenate([real_out, imag_out], axis=0))
    per = math.lcm(2 * chan, 128) // (2 * chan)
    per = per if width % per == 0 else width
    for m in range(0, width, per):
        taken = [
            take(wide, pl.ds(k * width + m + i, group, stride=rows), total_chan)
            for i in range(per)
            for k in range(2)
        ]
        for q in range(lons):
            piece = lanes([one[:, q * chan : (q + 1) * chan] for one in taken])
            lower = 2 * m * chan
            sent_ref[q, :, lower : lower + 2 * per * chan] = piece.astype(sent_ref.dtype)


def mix(got, weight, adjoint):
    lons, degrees, flat = got.shape
    total_chan = weight.shape[2]
    rows = flat * lons // total_chan
    group = 16 if degrees % 16 == 0 else degrees
    return pl.pallas_call(
        lambda *refs: mix_kernel(adjoint, *refs),
        grid=(degrees // group,),
        in_specs=[
            pl.BlockSpec((lons, group, flat), lambda step: (0, step, 0)),
            pl.BlockSpec((group, 2, total_chan, total_chan), lambda step: (step, 0, 0, 0)),
        ],
        out_specs=[
            pl.BlockSpec((lons, group, flat), lambda step: (0, step, 0)),
            pl.BlockSpec((group, rows, total_chan), lambda step: (step, 0, 0)),
        ],
        out_shape=[
            jax.ShapeDtypeStruct(got.shape, got.dtype),
            jax.ShapeDtypeStruct((degrees, rows, total_chan), got.dtype),
        ],
        scratch_shapes=[pltpu.VMEM((tiles(total_chan), group * rows, 128), jnp.float32)],
        **limits(4 * degrees * rows * total_chan**2, 2 * (weight.size + 3 * got.size)),
    )(got, weight)


def term_kernel(chunks, *refs):
    out_ref = refs[-1]
    chan = out_ref.shape[0]

    def over_rows(left, right):
        return lax.dot_general(
            left, right, (((0,), (0,)), ((), ())), preferred_element_type=jnp.float32
        )

    for index in range(refs[0].shape[0]):
        real_term = jnp.zeros((chan, chan), jnp.float32)
        imag_term = jnp.zeros((chan, chan), jnp.float32)
        for chunk in range(chunks):
            spec = refs[chunk][index]
            grad = refs[chunks + chunk][index]
            half = spec.shape[0] // 2
            wide = spec.astype(jnp.float32)
            turned = jnp.concatenate([-wide[half:], wide[:half]], axis=0).astype(spec.dtype)
            real_term += over_rows(grad, spec)
            imag_term += over_rows(grad, turned)
        both = jnp.concatenate([real_term, imag_term], axis=1)
        out_ref[:, 2 * chan * index : 2 * chan * (index + 1)] = both.astype(out_ref.dtype)


def weight_terms(specs, grads):
    degrees, rows, chan = specs[0].shape
    chunks = len(specs)
    group = group_of(degrees, 8)
    return pl.pallas_call(
        lambda *refs: term_kernel(chunks, *refs),
        grid=(degrees // group,),
        in_specs=[pl.BlockSpec((group, rows, chan), lambda step: (step, 0, 0))] * (2 * chunks),
        out_specs=pl.BlockSpec((chan, group * 2 * chan), lambda step: (0, step)),
        out_shape=jax.ShapeDtypeStruct((chan, degrees * 2 * chan), specs[0].dtype),
        compiler_params=pltpu.CompilerParams(vmem_limit_bytes=32 * 1024 * 1024),
        cost_estimate=pl.CostEstimate(
            flops=4 * chunks * degrees * rows * chan * chan,
            bytes_accessed=4 * degrees * chan * (chunks * rows + chan),
            transcendentals=0,
        ),
    )(*specs, *grads)


def on_device(field, cotangent, legendre, spectral_weight):
    lats = lax.axis_size("lat")
    lons = lax.axis_size("lon")
    chan, rows, longitudes = field.shape
    waves_here, degrees_here, latitudes = legendre.shape
    total_chan = chan * lons
    degrees = degrees_here * lons
    total_waves = waves_here * lats
    chunks = 2 if waves_here % 16 == 0 else 1
    width = waves_here // chunks
    fourier = jnp.asarray(wave_table(longitudes, total_waves))
    f32 = jnp.float32
    bf16 = jnp.bfloat16

    tables = [
        lax.all_gather(legendre[j * width : (j + 1) * width], "lon", axis=1, tiled=True)
        for j in range(chunks)
    ]

    def to_waves(grid):
        flat = grid.reshape(chan * rows, longitudes)
        local = lax.dot_general(fourier, flat, (((1,), (1,)), ((), ())), preferred_element_type=f32)
        local = local.astype(bf16).reshape(lats, waves_here * 2, chan * rows)
        return gather_rows(swap(local, "lat"), chan)

    def to_grid(parts):
        got = jnp.concatenate(parts, axis=1)
        return lax.dot_general(
            got.reshape(total_waves * 2, chan * rows),
            fourier,
            (((0,), (0,)), ((), ())),
            preferred_element_type=f32,
        ).reshape(chan, rows, longitudes)

    waves = to_waves(field)
    grad_waves = to_waves(cotangent)
    table, waves, grad_waves = lax.optimization_barrier((tables[0], waves, grad_waves))
    hold = lax.optimization_barrier

    def forward(given, j):
        return analyse(table, given, lons, j * width)

    def finish(mixed, table):
        return synthesise(table, mixed, lats, chan)

    specs, grads, backs, grad_backs = [], [], [], []
    if chunks == 1:
        got, grad_got = exchange(0, (forward(waves, 0), "lon"), (forward(grad_waves, 0), "lon"))
        mixed, spec = mix(got, spectral_weight, False)
        grad_mixed, grad = mix(grad_got, spectral_weight, True)
        terms = weight_terms([spec], [grad])
        mixed, grad_mixed, terms = hold((mixed, grad_mixed, terms))
        mixed, grad_mixed = exchange(1, (mixed, "lon"), (grad_mixed, "lon"))
        back, grad_back = finish(mixed, table), finish(grad_mixed, table)
        back, grad_back = exchange(2, (back, "lat"), (grad_back, "lat"))
        backs, grad_backs = [back], [grad_back]
    else:
        got, grad_got = exchange(0, (forward(waves, 0), "lon"), (forward(grad_waves, 0), "lon"))
        mixed, spec = mix(got, spectral_weight, False)
        grad_mixed, grad = mix(grad_got, spectral_weight, True)
        early = table
        table, mixed, grad_mixed = hold((tables[1], mixed, grad_mixed))
        late_got, late_grad_got = exchange(
            1, (forward(waves, 1), "lon"), (forward(grad_waves, 1), "lon")
        )
        mixed, grad_mixed, late_got, late_grad_got = hold(
            (mixed, grad_mixed, late_got, late_grad_got)
        )
        mixed = swap(mixed, "lon")
        late_mixed, late_spec = mix(late_got, spectral_weight, False)
        late_grad_mixed, late_grad = mix(late_grad_got, spectral_weight, True)
        terms = weight_terms([spec, late_spec], [grad, late_grad])
        mixed, grad_mixed, late_mixed, late_grad_mixed, terms = hold(
            (mixed, grad_mixed, late_mixed, late_grad_mixed, terms)
        )
        grad_mixed = swap(grad_mixed, "lon")
        back = finish(mixed, early)
        back, grad_mixed = hold((back, grad_mixed))
        grad_back = finish(grad_mixed, early)
        late_mixed, back, grad_back = exchange(
            2, (late_mixed, "lon"), (back, "lat"), (grad_back, "lat")
        )
        late_back = finish(late_mixed, table)
        late_grad_mixed, late_back = exchange(3, (late_grad_mixed, "lon"), (late_back, "lat"))
        late_grad_back = swap(finish(late_grad_mixed, table), "lat")
        backs, grad_backs = [back, late_back], [grad_back, late_grad_back]
    summed = lax.psum_scatter(terms, "lat", scatter_dimension=0, tiled=True)
    weight_grad = summed.reshape(-1, degrees_here, 2, total_chan).transpose(1, 2, 0, 3)
    output = (field.astype(f32) + to_grid(backs)).astype(bf16)
    field_grad = (cotangent.astype(f32) + to_grid(grad_backs)).astype(bf16)
    return (output, field_grad, weight_grad)


def solution(mesh):
    placed = (
        P("lon", "lat", None),
        P("lon", "lat", None),
        P("lat", "lon", None),
        P("lon", None, None, None),
    )
    return jax.shard_map(
        on_device,
        mesh=mesh,
        in_specs=placed,
        out_specs=(P("lon", "lat", None), P("lon", "lat", None), P("lon", None, "lat", None)),
        check_vma=False,
    )
```
